32 devices in a mesh: grp: 2 (over y), seq: 4 (over z), blk: 2 (over x), rep: 2 (over core).
Axes of the slice: x: 2, y: 2, z: 4, core: 2. Of those that a mesh axis runs over, the one named last changes fastest.
Arguments:
- q_proj: bfloat16 [8, 2048, 512], P(('grp', 'blk', 'rep'), 'seq'), parts along dimension 0, may hold values from -6 to 6
- k_proj: bfloat16 [8, 2048, 128], P(('grp', 'blk', 'rep'), 'seq'), parts along dimension 0, may hold values from -6 to 6
- v_proj: bfloat16 [8, 2048, 128], P(('grp', 'blk', 'rep'), 'seq'), parts along dimension 0, may hold values from -6 to 6
- q_gain: float32 [128], replicated, may hold values from 0.5 to 1.5
- k_gain: float32 [128], replicated, may hold values from 0.5 to 1.5
- out_weight: bfloat16 [512, 2560], P('seq'), may hold values from -0.25 to 0.25
- lengths: int32 [8, 1], P(('grp', 'blk', 'rep')), parts along dimension 0, may hold values from 512 to 2048, as said below
- query_emb: bfloat16 [512, 2560], P(('grp', 'blk')), parts along dimension 0, may hold values from -6 to 6
- teacher: float32 [512, 4], P(('grp', 'blk')), parts along dimension 0, may hold values from -16 to 16
Outputs:
- q_grad: bfloat16 [8, 2048, 512], P(('grp', 'blk', 'rep'), 'seq'), parts along dimension 0
- k_grad: bfloat16 [8, 2048, 128], P(('grp', 'blk', 'rep'), 'seq'), parts along dimension 0
- v_grad: bfloat16 [8, 2048, 128], P(('grp', 'blk', 'rep'), 'seq'), parts along dimension 0
- weight_grad: bfloat16 [1024, 2560], P(('grp', 'seq')), parts along dimension 0
- row_loss: float32 [512], P(('grp', 'blk')), parts along dimension 0
- col_loss: float32 [8], P('grp'), parts along dimension 0
The draws below stay inside these ranges and needn't reach their ends.
There are 2 independent parts, one for each index of `grp`. The reference program is written for one: setup_inputs(seed, part) draws one part's arguments, and reference() takes and returns one part's arrays. A program takes and returns all parts, laid end to end along the dimension named above; an argument that names none is the same for every part. Nothing has to cross between parts.
Inputs may be any that keep to these rules, and one draw needn't show every extreme that they name: `lengths`: live tokens of each passage, counted from its first position; the rest is padding.
All inputs are finite; a program needn't handle non-finite values.
Results may differ from the reference program's by a relative error of at most 0.017.
Values may be sent and summed in bfloat16 or wider, within the bound.
A program may use at most 64 MiB of HBM per device.

```python
import math
import jax
import jax.numpy as jnp
from jax import lax

E = 2560
HD = 128
GQA = 4
PASS_LEN = 2048
PASS_GRP = 1
HEADS = 4
KV_HEADS = 1
NGROUPS = 4
NPASS = 4
NQ = 256
GROUP_TOK = 2048


def draw_lengths(key, part):
    first_key, second_key = jax.random.split(jax.random.fold_in(key, 11))
    total = NGROUPS * PASS_GRP
    values = jax.random.randint(first_key, (total,), PASS_LEN // 4, PASS_LEN + 1)
    order = jax.random.permutation(second_key, total)
    values = values.at[order[0]].set(PASS_LEN).at[order[1]].set(PASS_LEN // 4)
    return values.reshape(NGROUPS, PASS_GRP).astype(jnp.int32)


def levels(key, shape, shards, smallest, top_value):
    gain, own = 1.0, jax.random.fold_in(key, 6)
    for dim, shards_of in shards:
        steps = jnp.exp(jax.random.uniform(jax.random.fold_in(own, dim), (shards_of,), jnp.float32, smallest / len(shards), top_value / len(shards)))
        gain = gain * jnp.repeat(steps, shape[dim] // shards_of).reshape([-1 if axis == dim else 1 for axis in range(len(shape))])
    return gain


def bell_draw(stream_key, dims, scale, most, shards=(), dtype=jnp.bfloat16):
    drawn = scale * jax.random.normal(stream_key, dims, jnp.float32)
    if shards:
        drawn = drawn * levels(stream_key, dims, shards, -0.22, 0.18)
    return jnp.clip(drawn, -most, most).astype(dtype)


def setup_inputs(seed: int = 0, part: int = 0) -> dict:
    keys = jax.random.split(jax.random.key(seed), 10)
    part_splits = jax.random.split(jax.random.fold_in(keys[9], part), 10)
    return {
        "q_proj": bell_draw(part_splits[0], (NGROUPS, GROUP_TOK, HEADS * HD), 1.0, 6.0, ((0, 4), (1, 4))),
        "k_proj": bell_draw(part_splits[1], (NGROUPS, GROUP_TOK, KV_HEADS * HD), 1.0, 6.0, ((0, 4), (1, 4))),
        "v_proj": bell_draw(part_splits[2], (NGROUPS, GROUP_TOK, KV_HEADS * HD), 1.0, 6.0, ((0, 4), (1, 4))),
        "q_gain": jnp.clip(1.0 + 0.1 * jax.random.normal(keys[3], (HD,), jnp.float32), 0.5, 1.5),
        "k_gain": jnp.clip(1.0 + 0.1 * jax.random.normal(keys[4], (HD,), jnp.float32), 0.5, 1.5),
        "out_weight": bell_draw(keys[5], (HEADS * HD, E), (HEADS * HD) ** -0.5, 0.25, ((0, 4),)),
        "lengths": draw_lengths(jax.random.fold_in(jax.random.fold_in(keys[9], part), 71), part),
        "query_emb": bell_draw(part_splits[7], (NQ, E), 1.0, 6.0, ((0, 2),)),
        "teacher": bell_draw(part_splits[8], (NQ, NPASS), 3.0, 16.0, ((0, 2),), jnp.float32),
    }


logit_divisor = 0.05

def rms_scale(wide):
    return lax.rsqrt(lax.optimization_barrier(jnp.mean(wide * wide, axis=-1, keepdims=True)) + 1e-06)

def normed(source, gain_weights):
    wide = source.astype(jnp.float32)
    return (wide * rms_scale(wide) * gain_weights).astype(jnp.bfloat16)

def norm_back(source, gain_weights, grad_out):
    wide = source.astype(jnp.float32)
    inv_rms = rms_scale(wide)
    scaled_grad = gain_weights * grad_out
    return (inv_rms * scaled_grad - wide * inv_rms ** 3 * lax.optimization_barrier(jnp.mean(scaled_grad * wide, axis=-1, keepdims=True))).astype(jnp.bfloat16)

def attention_weights(q_unit, k_unit):
    logits = jnp.dot(q_unit, k_unit.T, preferred_element_type=jnp.float32) * (1.0 / math.sqrt(HD))
    positions = lax.iota(jnp.int32, PASS_LEN)
    causal = positions[:, None] >= positions[None, :]
    powers = jnp.where(causal, jnp.exp(logits), 0.0)
    return lax.optimization_barrier((powers / lax.optimization_barrier(jnp.sum(powers, axis=1, keepdims=True))).astype(jnp.bfloat16))

def forward_core(q_unit, k_unit, value_rows, live_len):
    attend_b = attention_weights(q_unit, k_unit)
    positions = lax.iota(jnp.int32, PASS_LEN)
    live_mask = (positions < live_len).astype(jnp.bfloat16)
    col_weight = jnp.dot(live_mask, attend_b, preferred_element_type=jnp.float32) / live_len.astype(jnp.float32)
    pooled = lax.optimization_barrier(jnp.sum(col_weight[:, None] * value_rows.astype(jnp.float32), axis=0))
    return (pooled, col_weight.astype(jnp.bfloat16))

def group_heads(rows, heads):
    return rows.reshape(PASS_GRP, PASS_LEN, heads, HD).transpose(2, 0, 1, 3)

def reference(q_proj, k_proj, v_proj, q_gain, k_gain, out_weight, lengths, query_emb, teacher):
    inv_root = 1.0 / math.sqrt(HD)

    def prepare(q_rows, k_rows, v_rows):
        q_heads = group_heads(q_rows, HEADS)
        k_heads = jnp.repeat(group_heads(k_rows, KV_HEADS), GQA, axis=0)
        v_heads = jnp.repeat(group_heads(v_rows, KV_HEADS), GQA, axis=0)
        return (q_heads, k_heads, v_heads, normed(q_heads, q_gain), normed(k_heads, k_gain))

    def forward_group(pieces):
        q_rows, k_rows, v_rows, pass_lens = pieces
        q_heads, k_heads, v_heads, q_unit, k_unit = prepare(q_rows, k_rows, v_rows)

        def per_head(parts):
            return jax.vmap(forward_core)(parts[0], parts[1], parts[2], pass_lens)
        pooled, col_weight = lax.map(per_head, (q_unit, k_unit, v_heads))
        return (pooled.transpose(1, 0, 2).reshape(PASS_GRP, HEADS * HD), col_weight)
    pooled, col_weights = lax.map(forward_group, (q_proj, k_proj, v_proj, lengths))
    pooled_b = pooled.reshape(NPASS, HEADS * HD).astype(jnp.bfloat16)
    summed = jnp.dot(pooled_b, out_weight, preferred_element_type=jnp.float32)
    inv_norm = lax.rsqrt(lax.optimization_barrier(jnp.sum(summed * summed, axis=1, keepdims=True)) + 1e-06)
    passage_unit = summed * inv_norm
    document_representations = passage_unit.astype(jnp.bfloat16)
    query_wide = query_emb.astype(jnp.float32)
    request_unit_length = (query_wide * lax.rsqrt(lax.optimization_barrier(jnp.sum(query_wide * query_wide, axis=1, keepdims=True)) + 1e-06)).astype(jnp.bfloat16)
    learner_similarities = jnp.dot(request_unit_length, document_representations.T, preferred_element_type=jnp.float32) / logit_divisor
    exp_student = jnp.exp(learner_similarities)
    exp_teacher = jnp.exp(teacher)
    row_student = lax.optimization_barrier(jnp.sum(exp_student, axis=1, keepdims=True))
    row_teacher = lax.optimization_barrier(jnp.sum(exp_teacher, axis=1, keepdims=True))
    col_student = lax.optimization_barrier(jnp.sum(exp_student, axis=0))
    col_teacher = lax.optimization_barrier(jnp.sum(exp_teacher, axis=0))
    gap = exp_teacher * (teacher - learner_similarities)
    row_loss = lax.optimization_barrier(jnp.sum(gap, axis=1)) / row_teacher[:, 0] - jnp.log(row_teacher[:, 0]) + jnp.log(row_student[:, 0])
    col_loss = lax.optimization_barrier(jnp.sum(gap, axis=0)) / col_teacher - jnp.log(col_teacher) + jnp.log(col_student)
    similarity_derivative = ((exp_student / row_student - exp_teacher / row_teacher) / NQ + (exp_student / col_student - exp_teacher / col_teacher) / NPASS).astype(jnp.bfloat16)
    representation_derivative = jnp.dot(similarity_derivative.T, request_unit_length, preferred_element_type=jnp.float32) / logit_divisor
    grad_sum = ((representation_derivative - passage_unit * lax.optimization_barrier(jnp.sum(passage_unit * representation_derivative, axis=1, keepdims=True))) * inv_norm).astype(jnp.bfloat16)
    weight_grad = jnp.dot(pooled_b.T, grad_sum, preferred_element_type=jnp.float32).astype(jnp.bfloat16)
    grad_pool = jnp.dot(grad_sum, out_weight.T, preferred_element_type=jnp.float32)
    grad_pool = grad_pool.reshape(NGROUPS, PASS_GRP, HEADS, HD)

    def backward_core(q_unit, k_unit, value_rows, q_raw, k_raw, live_len, pool_grad):
        attend_w = attention_weights(q_unit, k_unit).astype(jnp.float32)
        positions = lax.iota(jnp.int32, PASS_LEN)
        live_mask = (positions < live_len).astype(jnp.float32) / live_len.astype(jnp.float32)
        value_dot = lax.optimization_barrier(jnp.sum(value_rows.astype(jnp.float32) * pool_grad[None, :], axis=1))
        mean_dot = jnp.dot(attend_w, value_dot, precision=lax.Precision.HIGHEST)
        grad_logits = (attend_w * live_mask[:, None] * (value_dot[None, :] - mean_dot[:, None]) * inv_root).astype(jnp.bfloat16)
        grad_q_unit = jnp.dot(grad_logits, k_unit, preferred_element_type=jnp.float32)
        grad_k_copy = jnp.dot(grad_logits.T, q_unit, preferred_element_type=jnp.float32)
        return (norm_back(q_raw, q_gain, grad_q_unit), norm_back(k_raw, k_gain, grad_k_copy))

    def merge_heads(terms):
        wide = terms.astype(jnp.float32).reshape(KV_HEADS, GQA, PASS_GRP, PASS_LEN, HD)
        merged = lax.optimization_barrier(jnp.sum(wide, axis=1)).astype(jnp.bfloat16)
        return merged.transpose(1, 2, 0, 3).reshape(GROUP_TOK, KV_HEADS * HD)

    def backward_group(pieces):
        q_rows, k_rows, v_rows, pass_lens, pool_grad, col_weight = pieces
        q_heads, k_heads, v_heads, q_unit, k_unit = prepare(q_rows, k_rows, v_rows)
        head_grads = pool_grad.transpose(1, 0, 2)

        def per_head(parts):
            return jax.vmap(backward_core)(parts[0], parts[1], parts[2], parts[3], parts[4], pass_lens, parts[5])
        q_terms, k_terms = lax.map(per_head, (q_unit, k_unit, v_heads, q_heads, k_heads, head_grads))
        v_terms = (col_weight.astype(jnp.float32)[..., None] * head_grads[:, :, None, :]).astype(jnp.bfloat16)
        q_out = q_terms.transpose(1, 2, 0, 3).reshape(GROUP_TOK, HEADS * HD)
        return (q_out, merge_heads(k_terms), merge_heads(v_terms))
    q_grad, k_grad, v_grad = lax.map(backward_group, (q_proj, k_proj, v_proj, lengths, grad_pool, col_weights))
    return (q_grad, k_grad, v_grad, weight_grad, row_loss, col_loss)
```

```python
import functools
import math

import jax
import jax.numpy as jnp
from jax import lax
from jax.experimental import pallas as pl
from jax.experimental.pallas import tpu as pltpu
from jax.sharding import PartitionSpec as P

HD = 128
LOGIT_DIVISOR = 0.05
INV_ROOT = 1.0 / math.sqrt(HD)
EXP2_SCALE = INV_ROOT * math.log2(math.e)
F32 = jnp.float32
BF16 = jnp.bfloat16
HIGHEST = lax.Precision.HIGHEST
NT = (((1,), (1,)), ((), ()))
TN = (((0,), (0,)), ((), ()))
NN = (((1,), (0,)), ((), ()))


def dot(a, b, dims, precision=None):
    return lax.dot_general(a, b, dims, precision=precision, preferred_element_type=F32)


def rms_scale(wide):
    return lax.rsqrt(jnp.mean(wide * wide, axis=-1, keepdims=True) + 1e-06)


def normed(source, gain):
    wide = source.astype(F32)
    return (wide * rms_scale(wide) * gain).astype(BF16)


def norm_back(source, gain, grad_out):
    wide = source.astype(F32)
    inv_rms = rms_scale(wide)
    scaled = gain * grad_out
    return (
        inv_rms * scaled - wide * inv_rms**3 * jnp.mean(scaled * wide, axis=-1, keepdims=True)
    ).astype(BF16)


def split_rows(row, rows=16):
    high = row.astype(BF16).astype(F32)
    low = row - high
    index = lax.broadcasted_iota(jnp.int32, (rows, row.shape[1]), 0)
    return jnp.where(index == 0, high, jnp.where(index == 1, low, 0.0)).astype(BF16)


def pad_rows(rows):
    missing = -rows.shape[0] % 8
    if missing:
        rows = jnp.concatenate([rows, jnp.zeros((missing, rows.shape[1]), F32)], axis=0)
    return rows


def loop(count, body):
    if isinstance(count, int) and count <= 4:
        for i in range(count):
            body(i)
    else:
        lax.fori_loop(0, count, lambda i, c: (body(i), c)[1], 0)


def kernel(
    cfg, q_ref, k_ref, v_ref, qg_ref, kg_ref, w_ref, len_ref, qe_ref, te_ref,
    qo_ref, ko_ref, vo_ref, wg_ref, rl_ref, cl_ref,
    qu, kall, pall, rs, coef, cwp, cwr, pps, ppr, sums, gps, vds, dkp, dkr, dqt, qea, tea,
    k_send, k_recv, c_send, c_recv, p_send, p_recv, s_send, s_recv, g_send, g_recv,
    v_send, v_recv, d_send, d_recv, e_send, e_recv, t_send, t_recv,
):
    n, nb, nr, tok, heads, kv, width, qb = cfg
    gqa = heads // kv
    npass = nb * nr
    total_q = nb * qb
    peers = n * npass
    s, b, r = lax.axis_index("seq"), lax.axis_index("blk"), lax.axis_index("rep")
    me_p = b * nr + r
    me = s * npass + me_p

    def coords(o):
        peer = lax.rem(me + o, peers)
        ps = peer // npass
        pp = lax.rem(peer, npass)
        return ps, pp, {"seq": ps, "blk": pp // nr, "rep": lax.rem(pp, nr)}

    def lanes(i):
        if isinstance(i, int):
            return slice(i * HD, (i + 1) * HD)
        return pl.ds(pl.multiple_of(i * HD, HD), HD)

    barrier = pltpu.get_barrier_semaphore()

    def greet(i):
        pl.semaphore_signal(
            barrier, inc=1, device_id=coords(i + 1)[2], device_id_type=pl.DeviceIdType.MESH
        )

    lax.fori_loop(0, peers - 1, lambda i, c: (greet(i), c)[1], 0)

    kg = kg_ref[...]
    qg = qg_ref[...]
    for g in range(kv):
        kall[s, g] = normed(k_ref[:, g * HD : (g + 1) * HD], kg)
    pl.semaphore_wait(barrier, peers - 1)

    def remote(src, dst, send, recv, device):
        return pltpu.make_async_remote_copy(
            src_ref=src, dst_ref=dst, send_sem=send, recv_sem=recv,
            device_id=device, device_id_type=pl.DeviceIdType.MESH,
        )

    def k_copy(dst, src):
        return remote(kall.at[src], kall.at[src], k_send.at[dst], k_recv.at[src], {"seq": dst})

    def c_copy(dst, src):
        return remote(cwp.at[dst], cwr.at[src], c_send.at[dst], c_recv.at[src], {"seq": dst})

    def d_copy(dst, src):
        return remote(dkp.at[dst], dkr.at[src], d_send.at[dst], d_recv.at[src], {"seq": dst})

    def v_copy(dst, src):
        return remote(vds.at[src], vds.at[src], v_send.at[dst], v_recv.at[src], {"seq": dst})

    def s_copy(dst, src):
        return remote(sums.at[src], sums.at[src], s_send.at[dst], s_recv.at[src], {"seq": dst})

    def g_copy(dst, src):
        return remote(gps.at[src], gps.at[src], g_send.at[dst], g_recv.at[src], {"seq": dst})

    def e_copy(dst, src):
        return remote(qe_ref, qea.at[src], e_send.at[dst], e_recv.at[src], {"blk": dst})

    def t_copy(dst, src):
        return remote(te_ref, tea.at[src], t_send.at[dst], t_recv.at[src], {"blk": dst})

    def p_copy(o, slot_s, slot_p, device, dst_head, index):
        return remote(
            pps.at[dst_head], ppr.at[slot_s, slot_p], p_send.at[index],
            p_recv.at[slot_s, slot_p], device,
        )

    def fori(lo, hi, body):
        lax.fori_loop(lo, hi, lambda i, c: (body(i), c)[1], 0)

    later = n - 1 - s
    fori(0, later, lambda i: k_copy(n - 1 - i, s).start())

    def other_blk(i):
        return lax.rem(b + 1 + i, nb)

    def other_seq(i):
        return lax.rem(s + 1 + i, n)

    for i in range(nb - 1):
        t_copy(other_blk(i), b).start()
        e_copy(other_blk(i), b).start()

    def q_norm(h):
        qu[h] = normed(q_ref[:, lanes(h)], qg)

    loop(heads, q_norm)

    def forward(j, diagonal):
        def one(h):
            logits = dot(kall[j, h // gqa], qu[h], NT)
            powers = jnp.exp2(logits * EXP2_SCALE)
            if diagonal:
                u = lax.broadcasted_iota(jnp.int32, powers.shape, 0)
                t = lax.broadcasted_iota(jnp.int32, powers.shape, 1)
                powers = jnp.where(u <= t, powers, 0.0)
            pall[j, h] = powers.astype(BF16)
            row = jnp.sum(powers, axis=0, keepdims=True)
            rs[h] = row if diagonal else rs[h] + row

        loop(heads, one)

    forward(s, True)

    def unit_queries(rows):
        wide = rows.astype(F32)
        return (
            wide * lax.rsqrt(jnp.sum(wide * wide, axis=1, keepdims=True) + 1e-06)
        ).astype(BF16)

    qea[b] = unit_queries(qe_ref[...])
    tea[b] = te_ref[...]

    def forward_step(i):
        j = s - 1 - i
        k_copy(s, j).wait_recv()
        forward(j, False)

    fori(0, s, forward_step)

    length = len_ref[0, 0]
    position = s * tok + lax.broadcasted_iota(jnp.int32, (1, tok), 1)
    live = jnp.where(position < length, 1.0, 0.0) / jnp.full((1, tok), length, jnp.int32).astype(F32)

    def weigh(h):
        coef[h] = live / rs[h]

    loop(heads, weigh)

    def column_step(i):
        def one(h):
            both = dot(split_rows(coef[h]), pall[i, h], NT)
            cwp[i, pl.ds(h, 1), :] = both[0:1] + both[1:2]

        loop(heads, one)

        @pl.when(i < s)
        def _():
            c_copy(i, s).start()

    fori(0, s + 1, column_step)

    def query_step(i):
        src = lax.rem(b + 1 + i, nb)
        t_copy(b, src).wait_recv()
        e_copy(b, src).wait_recv()
        qea[src] = unit_queries(qea[src])

    for i in range(nb - 1):
        query_step(i)

    cwr[s] = cwp[s]

    def column_add(i):
        src = s + 1 + i
        c_copy(s, src).wait_recv()
        cwr[s] = cwr[s] + cwr[src]

    fori(0, later, column_add)
    col_weight = cwr[s]
    for g in range(kv):
        part = dot(
            col_weight[g * gqa : (g + 1) * gqa],
            v_ref[:, g * HD : (g + 1) * HD].astype(F32), NN, HIGHEST,
        )
        for i in range(gqa):
            pps[g * gqa + i] = jnp.broadcast_to(part[i : i + 1], (8, HD))

    def p_start(i):
        ps, _, device = coords(i + 1)
        p_copy(i, s, me_p, device, ps, i).start()

    fori(0, peers - 1, p_start)
    ppr[s, me_p] = pps[s]

    def p_wait(i):
        ps, pp, device = coords(i + 1)
        p_copy(i, ps, pp, device, ps, i).wait_recv()

    fori(0, peers - 1, p_wait)
    rows = []
    for p in range(npass):
        row = ppr[0, p]
        for i in range(1, n):
            row = row + ppr[i, p]
        rows.append(row[0:1])
    pooled = jnp.concatenate(rows, axis=0).astype(BF16).astype(F32)
    part = dot(pooled.astype(BF16), w_ref[...], NN)
    fold = sums.shape[1] // npass
    fw = width // fold
    sums[s] = jnp.concatenate(
        [part[:, i * fw : (i + 1) * fw] for i in range(fold)], axis=0
    ).astype(BF16)
    fori(0, n - 1, lambda i: s_copy(other_seq(i), s).start())
    fori(0, n - 1, lambda i: s_copy(s, other_seq(i)).wait_recv())
    stacked = sums[0].astype(F32)
    for i in range(1, n):
        stacked = stacked + sums[i].astype(F32)
    summed = jnp.concatenate(
        [stacked[i * npass : (i + 1) * npass] for i in range(fold)], axis=1
    )

    inv_norm = lax.rsqrt(jnp.sum(summed * summed, axis=1, keepdims=True) + 1e-06)
    unit = summed * inv_norm
    emb = unit.astype(BF16)
    blocks = range(nb)
    score = [dot(emb, qea[i], NT) / LOGIT_DIVISOR for i in blocks]
    teach = [tea[i] for i in blocks]
    es = [jnp.exp(x) for x in score]
    et = [jnp.exp(x) for x in teach]
    gap = [et[i] * (teach[i] - score[i]) for i in blocks]
    zs = [jnp.sum(x, axis=0, keepdims=True) for x in es]
    zt = [jnp.sum(x, axis=0, keepdims=True) for x in et]
    cs = sum(jnp.sum(x, axis=1, keepdims=True) for x in es)
    ct = sum(jnp.sum(x, axis=1, keepdims=True) for x in et)
    cg = sum(jnp.sum(x, axis=1, keepdims=True) for x in gap)
    grad_emb = jnp.zeros((npass, width), F32)
    for i in blocks:
        ds = (es[i] / zs[i] - et[i] / zt[i]) / total_q + (es[i] / cs - et[i] / ct) / npass
        grad_emb = grad_emb + dot(ds.astype(BF16), qea[i], NN)
    grad_emb = grad_emb / LOGIT_DIVISOR
    grad_sum = (
        (grad_emb - unit * jnp.sum(unit * grad_emb, axis=1, keepdims=True)) * inv_norm
    ).astype(BF16)
    grad_pool = dot(grad_sum, w_ref[...], NT)
    index = lax.broadcasted_iota(jnp.int32, grad_pool.shape, 0)
    mine = jnp.sum(jnp.where(index == me_p, grad_pool, 0.0), axis=0, keepdims=True)
    gps[s] = jnp.broadcast_to(mine, (8, HD))
    fori(0, n - 1, lambda i: g_copy(other_seq(i), s).start())

    cl_ref[...] = cg / ct - jnp.log(ct) + jnp.log(cs)
    for i in blocks:

        @pl.when(b == i)
        def _():
            rl_ref[...] = (
                jnp.sum(gap[i], axis=0, keepdims=True) / zt[i] - jnp.log(zt[i]) + jnp.log(zs[i])
            )

    fori(0, n - 1, lambda i: g_copy(s, other_seq(i)).wait_recv())
    pool_grads = jnp.concatenate([gps[h, 0:1, :] for h in range(heads)], axis=0)
    for g in range(kv):
        vds[s, g * gqa : (g + 1) * gqa] = dot(
            pool_grads[g * gqa : (g + 1) * gqa],
            v_ref[:, g * HD : (g + 1) * HD].astype(F32), NT, HIGHEST,
        )
    fori(0, later, lambda i: v_copy(n - 1 - i, s).start())

    wg_ref[...] = dot(
        pad_rows(pooled).T.astype(BF16), pad_rows(grad_sum.astype(F32)).astype(BF16), NN
    ).astype(BF16)
    col_rounded = col_weight.astype(BF16).astype(F32)
    for g in range(kv):
        vo_ref[:, g * HD : (g + 1) * HD] = dot(
            pad_rows(col_rounded[g * gqa : (g + 1) * gqa]).T,
            pad_rows(pool_grads[g * gqa : (g + 1) * gqa]), NN, HIGHEST,
        ).astype(BF16)

    fori(0, s, lambda i: v_copy(s, i).wait_recv())

    def mean_head(h):
        def add(j, carry):
            both = dot(split_rows(vds[j, pl.ds(h, 1), :]), pall[j, h], NN)
            return carry + both[0:1] + both[1:2]

        rs[h] = lax.fori_loop(0, s + 1, add, jnp.zeros((1, tok), F32)) / rs[h]
        dqt[h] = jnp.zeros((HD, tok), F32)

    loop(heads, mean_head)

    def backward_step(j):
        def one_kv(g):
            columns = pad_rows(vds[j, pl.ds(g * gqa, gqa), :]).T
            total = jnp.zeros((tok, HD), F32)
            for i in range(gqa):
                h = g * gqa + i
                grad_logits = (
                    pall[j, h].astype(F32)
                    * (coef[h] * INV_ROOT)
                    * (columns[:, i : i + 1] - rs[h])
                ).astype(BF16)
                total = total + dot(grad_logits, qu[h], NN)
                dqt[h] = dqt[h] + dot(kall[j, g], grad_logits, TN)
            dkp[j, g] = total.astype(BF16)

        loop(kv, one_kv)

        @pl.when(j < s)
        def _():
            d_copy(j, s).start()

    fori(0, s + 1, backward_step)

    def q_out(h):
        qo_ref[:, lanes(h)] = norm_back(q_ref[:, lanes(h)], qg, dqt[h].T)

    loop(heads, q_out)

    fori(0, later, lambda i: d_copy(s, s + 1 + i).wait_recv())
    for g in range(kv):
        total = lax.fori_loop(
            0, later, lambda i, c: c + dkr[s + 1 + i, g].astype(F32), dkp[s, g].astype(F32)
        )
        ko_ref[:, g * HD : (g + 1) * HD] = norm_back(k_ref[:, g * HD : (g + 1) * HD], kg, total)

    fori(0, later, lambda i: k_copy(n - 1 - i, s).wait_send())
    fori(0, later, lambda i: v_copy(n - 1 - i, s).wait_send())
    for i in range(nb - 1):
        t_copy(other_blk(i), b).wait_send()
        e_copy(other_blk(i), b).wait_send()
    fori(0, s, lambda i: c_copy(i, s).wait_send())
    fori(0, s, lambda i: d_copy(i, s).wait_send())
    fori(0, n - 1, lambda i: s_copy(other_seq(i), s).wait_send())
    fori(0, n - 1, lambda i: g_copy(other_seq(i), s).wait_send())

    def p_done(i):
        ps, _, device = coords(i + 1)
        p_copy(i, s, me_p, device, ps, i).wait_send()

    fori(0, peers - 1, p_done)


def shards(q_proj, k_proj, v_proj, q_gain, k_gain, out_weight, lengths, query_emb, teacher):
    n, nb, nr = lax.axis_size("seq"), lax.axis_size("blk"), lax.axis_size("rep")
    tok = q_proj.shape[1]
    heads = q_proj.shape[2] // HD
    kv = k_proj.shape[2] // HD
    width = out_weight.shape[1]
    qb = query_emb.shape[0]
    npass = nb * nr
    assert out_weight.shape[0] == HD and heads == n and teacher.shape[1] == npass
    peers = n * npass
    fold = 4
    vmem = pl.BlockSpec(memory_space=pltpu.VMEM)
    smem = pl.BlockSpec(memory_space=pltpu.SMEM)
    sem = pltpu.SemaphoreType.DMA
    cfg = (n, nb, nr, tok, heads, kv, width, qb)
    outs = pl.pallas_call(
        functools.partial(kernel, cfg),
        out_shape=(
            jax.ShapeDtypeStruct((tok, heads * HD), BF16),
            jax.ShapeDtypeStruct((tok, kv * HD), BF16),
            jax.ShapeDtypeStruct((tok, kv * HD), BF16),
            jax.ShapeDtypeStruct((HD, width), BF16),
            jax.ShapeDtypeStruct((1, qb), F32),
            jax.ShapeDtypeStruct((npass, 1), F32),
        ),
        in_specs=[vmem] * 6 + [smem] + [vmem] * 2,
        out_specs=(vmem,) * 6,
        scratch_shapes=[
            pltpu.VMEM((heads, tok, HD), BF16),
            pltpu.VMEM((n, kv, tok, HD), BF16),
            pltpu.VMEM((n, heads, tok, tok), BF16),
            pltpu.VMEM((heads, 1, tok), F32),
            pltpu.VMEM((heads, 1, tok), F32),
            pltpu.VMEM((n, heads, tok), F32),
            pltpu.VMEM((n, heads, tok), F32),
            pltpu.VMEM((heads, 8, HD), F32),
            pltpu.VMEM((n, npass, 8, HD), F32),
            pltpu.VMEM((n, npass * fold, width // fold), BF16),
            pltpu.VMEM((n, 8, HD), F32),
            pltpu.VMEM((n, heads, tok), F32),
            pltpu.VMEM((n, kv, tok, HD), BF16),
            pltpu.VMEM((n, kv, tok, HD), BF16),
            pltpu.VMEM((heads, HD, tok), F32),
            pltpu.VMEM((nb, qb, width), BF16),
            pltpu.VMEM((nb, npass, qb), F32),
            sem((n,)), sem((n,)), sem((n,)), sem((n,)),
            sem((peers,)), sem((n, npass)),
            sem((n,)), sem((n,)), sem((n,)), sem((n,)),
            sem((n,)), sem((n,)), sem((n,)), sem((n,)),
            sem((nb,)), sem((nb,)), sem((nb,)), sem((nb,)),
        ],
        compiler_params=pltpu.CompilerParams(
            collective_id=0, has_side_effects=True, vmem_limit_bytes=58 * 2**20
        ),
    )(
        q_proj[0], k_proj[0], v_proj[0], q_gain[None], k_gain[None], out_weight, lengths,
        query_emb, teacher.T,
    )
    q_grad, k_grad, v_grad, weight_grad, row_loss, col_loss = outs
    return q_grad[None], k_grad[None], v_grad[None], weight_grad, row_loss[0], col_loss[:, 0]


def solution(mesh):
    placed = (
        P(("grp", "blk", "rep"), "seq", None),
        P(("grp", "blk", "rep"), "seq", None),
        P(("grp", "blk", "rep"), "seq", None),
        P(),
        P(),
        P("seq", None),
        P(("grp", "blk", "rep"), None),
        P(("grp", "blk"), None),
        P(("grp", "blk"), None),
    )
    return jax.shard_map(
        shards,
        mesh=mesh,
        in_specs=placed,
        out_specs=(
            P(("grp", "blk", "rep"), "seq", None),
            P(("grp", "blk", "rep"), "seq", None),
            P(("grp", "blk", "rep"), "seq", None),
            P(("grp", "seq"), None),
            P(("grp", "blk")),
            P("grp"),
        ),
        check_vma=False,
    )
```

```python
import functools
import math

import jax
import jax.numpy as jnp
from jax import lax
from jax.experimental import pallas as pl
from jax.experimental.pallas import tpu as pltpu
from jax.sharding import PartitionSpec as P

HD = 128
LOGIT_DIVISOR = 0.05
INV_ROOT = 1.0 / math.sqrt(HD)
EXP2_SCALE = INV_ROOT * math.log2(math.e)
F32 = jnp.float32
BF16 = jnp.bfloat16
HIGHEST = lax.Precision.HIGHEST
NT = (((1,), (1,)), ((), ()))
TN = (((0,), (0,)), ((), ()))
NN = (((1,), (0,)), ((), ()))


def dot(a, b, dims, precision=None):
    return lax.dot_general(a, b, dims, precision=precision, preferred_element_type=F32)


def rms_scale(wide):
    return lax.rsqrt(jnp.mean(wide * wide, axis=-1, keepdims=True) + 1e-06)


def normed(source, gain):
    wide = source.astype(F32)
    return (wide * rms_scale(wide) * gain).astype(BF16)


def norm_back(source, gain, grad_out):
    wide = source.astype(F32)
    inv_rms = rms_scale(wide)
    scaled = gain * grad_out
    return (
        inv_rms * scaled - wide * inv_rms**3 * jnp.mean(scaled * wide, axis=-1, keepdims=True)
    ).astype(BF16)


def split_rows(row, rows=16):
    high = row.astype(BF16).astype(F32)
    low = row - high
    index = lax.broadcasted_iota(jnp.int32, (rows, row.shape[1]), 0)
    return jnp.where(index == 0, high, jnp.where(index == 1, low, 0.0)).astype(BF16)


def pad_rows(rows):
    missing = -rows.shape[0] % 8
    if missing:
        rows = jnp.concatenate([rows, jnp.zeros((missing, rows.shape[1]), F32)], axis=0)
    return rows


def loop(count, body):
    if isinstance(count, int) and count <= 4:
        for i in range(count):
            body(i)
    else:
        lax.fori_loop(0, count, lambda i, c: (body(i), c)[1], 0)


def kernel(
    cfg, q_hbm, k_hbm, v_hbm, qg_ref, kg_ref, w_hbm, len_ref, qe_hbm, te_ref,
    qo_hbm, ko_hbm, vo_hbm, wg_hbm, rl_ref, cl_ref,
    q_ref, k_ref, v_ref, w_ref, qo_ref, ko_ref, vo_ref, wg_ref, in_sem, out_sem, qer, h_send, f_send,
    qu, kall, pall, rs, coef, cwp, cwr, pps, ppr, sums, gps, vds, dkp, dkr, dkf, dqt, qea, tea,
    k_send, k_recv, c_send, c_recv, p_send, p_recv, s_send, s_recv, g_send, g_recv,
    v_send, v_recv, d_send, d_recv, e_send, e_recv, t_send, t_recv,
):
    n, nb, nr, tok, heads, kv, width, qb = cfg
    gqa = heads // kv
    npass = nb * nr
    total_q = nb * qb
    peers = n * npass
    s, b, r = lax.axis_index("seq"), lax.axis_index("blk"), lax.axis_index("rep")
    me_p = b * nr + r
    me = s * npass + me_p

    def coords(o):
        peer = lax.rem(me + o, peers)
        ps = peer // npass
        pp = lax.rem(peer, npass)
        return ps, pp, {"seq": ps, "blk": pp // nr, "rep": lax.rem(pp, nr)}

    def lanes(i):
        if isinstance(i, int):
            return slice(i * HD, (i + 1) * HD)
        return pl.ds(pl.multiple_of(i * HD, HD), HD)

    def fori(lo, hi, body):
        lax.fori_loop(lo, hi, lambda i, c: (body(i), c)[1], 0)

    barrier = pltpu.get_barrier_semaphore()

    def greet(i):
        pl.semaphore_signal(
            barrier, inc=1, device_id=coords(i + 1)[2], device_id_type=pl.DeviceIdType.MESH
        )

    lax.fori_loop(0, peers - 1, lambda i, c: (greet(i), c)[1], 0)

    loads = [
        pltpu.make_async_copy(src, dst, in_sem.at[i])
        for i, (src, dst) in enumerate([
            (k_hbm, k_ref), (q_hbm, q_ref), (qe_hbm, qer.at[b]), (v_hbm, v_ref), (w_hbm, w_ref)
        ])
    ]
    for load in loads:
        load.start()
    stores = [
        pltpu.make_async_copy(src, dst, out_sem.at[i])
        for i, (src, dst) in enumerate([
            (qo_ref, qo_hbm), (ko_ref, ko_hbm), (vo_ref, vo_hbm), (wg_ref, wg_hbm)
        ])
    ]
    kg = kg_ref[...]
    qg = qg_ref[...]
    loads[0].wait()
    for g in range(kv):
        kall[s, g] = normed(k_ref[:, g * HD : (g + 1) * HD], kg)
    loads[1].wait()

    def q_norm(h):
        qu[h] = normed(q_ref[:, lanes(h)], qg)

    loop(heads, q_norm)
    loads[2].wait()
    pl.semaphore_wait(barrier, peers - 1)

    def remote(src, dst, send, recv, device):
        return pltpu.make_async_remote_copy(
            src_ref=src, dst_ref=dst, send_sem=send, recv_sem=recv,
            device_id=device, device_id_type=pl.DeviceIdType.MESH,
        )

    even = lax.rem(s, 2) == 0
    partner = s + 1 - 2 * lax.rem(s, 2)

    def k_copy(dst, j):
        return remote(kall.at[j], kall.at[j], k_send.at[dst], k_recv.at[j], {"seq": dst})

    def k_pass(j):
        return remote(kall.at[j], kall.at[j], f_send.at[j], k_recv.at[j], {"seq": partner})

    def k_wait(j):
        k_copy(s, j).wait_recv()

    evens = (n - 1 - s) // 2

    def even_after(i):
        return n - 2 - 2 * i

    def k_start():
        fori(0, evens, lambda i: k_copy(even_after(i), s).start())

        @pl.when(even)
        def _():
            k_pass(s).start()

    def c_copy(dst, src):
        return remote(cwp.at[dst], cwr.at[src], c_send.at[dst], c_recv.at[src], {"seq": dst})

    def d_copy(dst, src):
        return remote(dkp.at[dst], dkr.at[src], d_send.at[dst], d_recv.at[src], {"seq": dst})

    def v_copy(dst, src):
        return remote(vds.at[src], vds.at[src], v_send.at[dst], v_recv.at[src], {"seq": dst})

    def s_copy(dst, src):
        return remote(sums.at[src], sums.at[src], s_send.at[dst], s_recv.at[src], {"seq": dst})

    def g_copy(dst, src):
        return remote(gps.at[src], gps.at[src], g_send.at[dst], g_recv.at[src], {"seq": dst})

    half = qb // nr

    def e_copy(dst, src):
        part = pl.ds(pl.multiple_of(r * half, half), half)
        return remote(
            qer.at[b, part], qer.at[src, part], e_send.at[dst], e_recv.at[src, r], {"blk": dst}
        )

    def h_copy(src, i):
        part = pl.ds(pl.multiple_of(r * half, half), half)
        return remote(
            qer.at[src, part], qer.at[src, part], h_send.at[src, i], e_recv.at[src, r],
            {"rep": lax.rem(r + 1 + i, nr)},
        )

    def h_wait(src, i):
        other = lax.rem(r + 1 + i, nr)
        part = pl.ds(pl.multiple_of(other * half, half), half)
        remote(
            qer.at[src, part], qer.at[src, part], h_send.at[src, i], e_recv.at[src, other],
            {"rep": other},
        ).wait_recv()

    def t_copy(dst, src):
        return remote(te_ref, tea.at[src], t_send.at[dst], t_recv.at[src], {"blk": dst})

    def p_copy(o, slot_s, slot_p, device, dst_head, index):
        return remote(
            pps.at[dst_head], ppr.at[slot_s, slot_p], p_send.at[index],
            p_recv.at[slot_s, slot_p], device,
        )

    later = n - 1 - s
    k_start()

    def other_blk(i):
        return lax.rem(b + 1 + i, nb)

    def other_seq(i):
        return lax.rem(s + 1 + i, n)

    for i in range(nb - 1):
        t_copy(other_blk(i), b).start()
        e_copy(other_blk(i), b).start()

    def forward(j, diagonal):
        def one(h):
            logits = dot(kall[j, h // gqa], qu[h], NT)
            powers = jnp.exp2(logits * EXP2_SCALE)
            if diagonal:
                u = lax.broadcasted_iota(jnp.int32, powers.shape, 0)
                t = lax.broadcasted_iota(jnp.int32, powers.shape, 1)
                powers = jnp.where(u <= t, powers, 0.0)
            pall[j, h] = powers.astype(BF16)
            row = jnp.sum(powers, axis=0, keepdims=True)
            rs[h] = row if diagonal else rs[h] + row

        loop(heads, one)

    forward(s, True)

    def unit_queries(rows):
        wide = rows.astype(F32)
        return (
            wide * lax.rsqrt(jnp.sum(wide * wide, axis=1, keepdims=True) + 1e-06)
        ).astype(BF16)

    qea[b] = unit_queries(qer[b])
    tea[b] = te_ref[...]

    def forward_step(i):
        j = s - 1 - i
        k_wait(j)

        @pl.when(even)
        def _():
            k_pass(j).start()

        forward(j, False)

    fori(0, s, forward_step)

    for i in range(nb - 1):
        src = other_blk(i)
        e_copy(b, src).wait_recv()
        for o in range(nr - 1):
            h_copy(src, o).start()

    length = len_ref[0, 0]
    position = s * tok + lax.broadcasted_iota(jnp.int32, (1, tok), 1)
    live = jnp.where(position < length, 1.0, 0.0) / jnp.full((1, tok), length, jnp.int32).astype(F32)

    def weigh(h):
        coef[h] = live / rs[h]

    loop(heads, weigh)

    def column_step(i):
        def one(h):
            both = dot(split_rows(coef[h]), pall[i, h], NT)
            cwp[i, pl.ds(h, 1), :] = both[0:1] + both[1:2]

        loop(heads, one)

        @pl.when(i < s)
        def _():
            c_copy(i, s).start()

    fori(0, s + 1, column_step)

    def query_step(i):
        src = lax.rem(b + 1 + i, nb)
        t_copy(b, src).wait_recv()
        for o in range(nr - 1):
            h_wait(src, o)
        qea[src] = unit_queries(qer[src])

    for i in range(nb - 1):
        query_step(i)

    cwr[s] = cwp[s]

    def column_add(i):
        src = s + 1 + i
        c_copy(s, src).wait_recv()
        cwr[s] = cwr[s] + cwr[src]

    fori(0, later, column_add)
    col_weight = cwr[s]
    loads[3].wait()
    for g in range(kv):
        part = dot(
            col_weight[g * gqa : (g + 1) * gqa],
            v_ref[:, g * HD : (g + 1) * HD].astype(F32), NN, HIGHEST,
        )
        for i in range(gqa):
            pps[g * gqa + i] = jnp.broadcast_to(part[i : i + 1], (8, HD))

    def p_start(i):
        ps, _, device = coords(i + 1)
        p_copy(i, s, me_p, device, ps, i).start()

    fori(0, peers - 1, p_start)
    ppr[s, me_p] = pps[s]

    def p_wait(i):
        ps, pp, device = coords(i + 1)
        p_copy(i, ps, pp, device, ps, i).wait_recv()

    fori(0, peers - 1, p_wait)
    rows = []
    for p in range(npass):
        row = ppr[0, p]
        for i in range(1, n):
            row = row + ppr[i, p]
        rows.append(row[0:1])
    loads[4].wait()
    pooled = jnp.concatenate(rows, axis=0).astype(BF16).astype(F32)
    part = dot(pooled.astype(BF16), w_ref[...], NN)
    fold = sums.shape[1] // npass
    fw = width // fold
    sums[s] = jnp.concatenate(
        [part[:, i * fw : (i + 1) * fw] for i in range(fold)], axis=0
    ).astype(BF16)
    fori(0, n - 1, lambda i: s_copy(other_seq(i), s).start())
    fori(0, n - 1, lambda i: s_copy(s, other_seq(i)).wait_recv())
    stacked = sums[0].astype(F32)
    for i in range(1, n):
        stacked = stacked + sums[i].astype(F32)
    summed = jnp.concatenate(
        [stacked[i * npass : (i + 1) * npass] for i in range(fold)], axis=1
    )

    inv_norm = lax.rsqrt(jnp.sum(summed * summed, axis=1, keepdims=True) + 1e-06)
    unit = summed * inv_norm
    emb = unit.astype(BF16)
    blocks = range(nb)
    score = [dot(emb, qea[i], NT) / LOGIT_DIVISOR for i in blocks]
    teach = [tea[i] for i in blocks]
    es = [jnp.exp(x) for x in score]
    et = [jnp.exp(x) for x in teach]
    gap = [et[i] * (teach[i] - score[i]) for i in blocks]
    zs = [jnp.sum(x, axis=0, keepdims=True) for x in es]
    zt = [jnp.sum(x, axis=0, keepdims=True) for x in et]
    cs = sum(jnp.sum(x, axis=1, keepdims=True) for x in es)
    ct = sum(jnp.sum(x, axis=1, keepdims=True) for x in et)
    cg = sum(jnp.sum(x, axis=1, keepdims=True) for x in gap)
    grad_emb = jnp.zeros((npass, width), F32)
    for i in blocks:
        ds = (es[i] / zs[i] - et[i] / zt[i]) / total_q + (es[i] / cs - et[i] / ct) / npass
        grad_emb = grad_emb + dot(ds.astype(BF16), qea[i], NN)
    grad_emb = grad_emb / LOGIT_DIVISOR
    grad_sum = (
        (grad_emb - unit * jnp.sum(unit * grad_emb, axis=1, keepdims=True)) * inv_norm
    ).astype(BF16)
    grad_pool = dot(grad_sum, w_ref[...], NT)
    index = lax.broadcasted_iota(jnp.int32, grad_pool.shape, 0)
    mine = jnp.sum(jnp.where(index == me_p, grad_pool, 0.0), axis=0, keepdims=True)
    gps[s] = jnp.broadcast_to(mine, (8, HD))
    fori(0, n - 1, lambda i: g_copy(other_seq(i), s).start())

    col_loss = cg / ct - jnp.log(ct) + jnp.log(cs)
    square = [lax.broadcasted_iota(jnp.int32, (npass, npass), i) for i in range(2)]
    cl_ref[...] = jnp.sum(
        jnp.where(square[0] == square[1], col_loss, 0.0), axis=0, keepdims=True
    )
    for i in blocks:

        @pl.when(b == i)
        def _():
            rl_ref[...] = (
                jnp.sum(gap[i], axis=0, keepdims=True) / zt[i] - jnp.log(zt[i]) + jnp.log(zs[i])
            )

    fori(0, n - 1, lambda i: g_copy(s, other_seq(i)).wait_recv())
    pool_grads = jnp.concatenate([gps[h, 0:1, :] for h in range(heads)], axis=0)
    for g in range(kv):
        vds[s, g * gqa : (g + 1) * gqa] = dot(
            pool_grads[g * gqa : (g + 1) * gqa],
            v_ref[:, g * HD : (g + 1) * HD].astype(F32), NT, HIGHEST,
        )
    fori(0, later, lambda i: v_copy(n - 1 - i, s).start())

    wg_ref[...] = dot(
        pad_rows(pooled).T.astype(BF16), pad_rows(grad_sum.astype(F32)).astype(BF16), NN
    ).astype(BF16)
    col_rounded = col_weight.astype(BF16).astype(F32)
    for g in range(kv):
        vo_ref[:, g * HD : (g + 1) * HD] = dot(
            pad_rows(col_rounded[g * gqa : (g + 1) * gqa]).T,
            pad_rows(pool_grads[g * gqa : (g + 1) * gqa]), NN, HIGHEST,
        ).astype(BF16)

    stores[3].start()
    stores[2].start()

    fori(0, s, lambda i: v_copy(s, i).wait_recv())

    def mean_head(h):
        def add(j, carry):
            both = dot(split_rows(vds[j, pl.ds(h, 1), :]), pall[j, h], NN)
            return carry + both[0:1] + both[1:2]

        rs[h] = lax.fori_loop(0, s + 1, add, jnp.zeros((1, tok), F32)) / rs[h]
        dqt[h] = jnp.zeros((HD, tok), F32)

    loop(heads, mean_head)

    def backward_step(j):
        def one_kv(g):
            columns = pad_rows(vds[j, pl.ds(g * gqa, gqa), :]).T
            total = jnp.zeros((tok, HD), F32)
            for i in range(gqa):
                h = g * gqa + i
                grad_logits = (
                    pall[j, h].astype(F32)
                    * (coef[h] * INV_ROOT)
                    * (columns[:, i : i + 1] - rs[h])
                ).astype(BF16)
                total = total + dot(grad_logits, qu[h], NN)
                dqt[h] = dqt[h] + dot(kall[j, g], grad_logits, TN)
            dkf[g] = total

        loop(kv, one_kv)

    def send_step(j):
        backward_step(j)

        for g in range(kv):
            dkp[j, g] = dkf[g].astype(BF16)
        d_copy(j, s).start()

    fori(0, s, send_step)
    backward_step(s)

    def q_out(h):
        qo_ref[:, lanes(h)] = norm_back(q_ref[:, lanes(h)], qg, dqt[h].T)

    loop(heads, q_out)
    stores[0].start()

    def d_add(i):
        src = n - 1 - i
        d_copy(s, src).wait_recv()
        for g in range(kv):
            dkf[g] = dkf[g] + dkr[src, g].astype(F32)

    fori(0, later, d_add)

    for g in range(kv):
        ko_ref[:, g * HD : (g + 1) * HD] = norm_back(k_ref[:, g * HD : (g + 1) * HD], kg, dkf[g])
    stores[1].start()

    fori(0, evens, lambda i: k_copy(even_after(i), s).wait_send())

    @pl.when(even)
    def _():
        fori(0, s + 1, lambda i: k_pass(i).wait_send())

    fori(0, later, lambda i: v_copy(n - 1 - i, s).wait_send())
    for i in range(nb - 1):
        t_copy(other_blk(i), b).wait_send()
        e_copy(other_blk(i), b).wait_send()
        for o in range(nr - 1):
            h_copy(other_blk(i), o).wait_send()
    fori(0, s, lambda i: c_copy(i, s).wait_send())
    fori(0, s, lambda i: d_copy(i, s).wait_send())
    fori(0, n - 1, lambda i: s_copy(other_seq(i), s).wait_send())
    fori(0, n - 1, lambda i: g_copy(other_seq(i), s).wait_send())

    def p_done(i):
        ps, _, device = coords(i + 1)
        p_copy(i, s, me_p, device, ps, i).wait_send()

    fori(0, peers - 1, p_done)
    for store in stores:
        store.wait()


def finish(*refs):
    count = len(refs) // 2
    for i in range(count):
        refs[count + i][...] = refs[i][...]


def shards(q_proj, k_proj, v_proj, q_gain, k_gain, out_weight, lengths, query_emb, teacher):
    n, nb, nr = lax.axis_size("seq"), lax.axis_size("blk"), lax.axis_size("rep")
    tok = q_proj.shape[1]
    heads = q_proj.shape[2] // HD
    kv = k_proj.shape[2] // HD
    width = out_weight.shape[1]
    qb = query_emb.shape[0]
    npass = nb * nr
    assert out_weight.shape[0] == HD and heads == n and n % 2 == 0 and teacher.shape[1] == npass
    peers = n * npass
    fold = 4
    vmem = pl.BlockSpec(memory_space=pltpu.VMEM)
    hbm = pl.BlockSpec(memory_space=pl.ANY)
    smem = pl.BlockSpec(memory_space=pltpu.SMEM)
    sem = pltpu.SemaphoreType.DMA
    cfg = (n, nb, nr, tok, heads, kv, width, qb)
    outs = pl.pallas_call(
        functools.partial(kernel, cfg),
        out_shape=(
            jax.ShapeDtypeStruct((tok, heads * HD), BF16),
            jax.ShapeDtypeStruct((tok, kv * HD), BF16),
            jax.ShapeDtypeStruct((tok, kv * HD), BF16),
            jax.ShapeDtypeStruct((HD, width), BF16),
            jax.ShapeDtypeStruct((1, qb), F32),
            jax.ShapeDtypeStruct((1, npass), F32),
        ),
        in_specs=[hbm] * 3 + [vmem] * 2 + [hbm, smem, hbm, vmem],
        out_specs=(hbm,) * 4 + (vmem,) * 2,
        scratch_shapes=[
            pltpu.VMEM((tok, heads * HD), BF16),
            pltpu.VMEM((tok, kv * HD), BF16),
            pltpu.VMEM((tok, kv * HD), BF16),
            pltpu.VMEM((HD, width), BF16),
            pltpu.VMEM((tok, heads * HD), BF16),
            pltpu.VMEM((tok, kv * HD), BF16),
            pltpu.VMEM((tok, kv * HD), BF16),
            pltpu.VMEM((HD, width), BF16),
            sem((5,)), sem((4,)),
            pltpu.VMEM((nb, qb, width), BF16),
            sem((nb, nr)), sem((n,)),
            pltpu.VMEM((heads, tok, HD), BF16),
            pltpu.VMEM((n, kv, tok, HD), BF16),
            pltpu.VMEM((n, heads, tok, tok), BF16),
            pltpu.VMEM((heads, 1, tok), F32),
            pltpu.VMEM((heads, 1, tok), F32),
            pltpu.VMEM((n, heads, tok), F32),
            pltpu.VMEM((n, heads, tok), F32),
            pltpu.VMEM((heads, 8, HD), F32),
            pltpu.VMEM((n, npass, 8, HD), F32),
            pltpu.VMEM((n, npass * fold, width // fold), BF16),
            pltpu.VMEM((n, 8, HD), F32),
            pltpu.VMEM((n, heads, tok), F32),
            pltpu.VMEM((n, kv, tok, HD), BF16),
            pltpu.VMEM((n, kv, tok, HD), BF16),
            pltpu.VMEM((kv, tok, HD), F32),
            pltpu.VMEM((heads, HD, tok), F32),
            pltpu.VMEM((nb, qb, width), BF16),
            pltpu.VMEM((nb, npass, qb), F32),
            sem((n,)), sem((n,)), sem((n,)), sem((n,)),
            sem((peers,)), sem((n, npass)),
            sem((n,)), sem((n,)), sem((n,)), sem((n,)),
            sem((n,)), sem((n,)), sem((n,)), sem((n,)),
            sem((nb,)), sem((nb, nr)), sem((nb,)), sem((nb,)),
        ],
        compiler_params=pltpu.CompilerParams(
            collective_id=0, has_side_effects=True, vmem_limit_bytes=58 * 2**20
        ),
    )(
        q_proj[0], k_proj[0], v_proj[0], q_gain[None], k_gain[None], out_weight, lengths,
        query_emb, teacher.T,
    )
    outs = pl.pallas_call(
        finish,
        out_shape=tuple(jax.ShapeDtypeStruct(x.shape, x.dtype) for x in outs),
        in_specs=[vmem] * len(outs),
        out_specs=(vmem,) * len(outs),
    )(*outs)
    q_grad, k_grad, v_grad, weight_grad, row_loss, col_loss = outs
    return q_grad[None], k_grad[None], v_grad[None], weight_grad, row_loss[0], col_loss[0]


def solution(mesh):
    placed = (
        P(("grp", "blk", "rep"), "seq", None),
        P(("grp", "blk", "rep"), "seq", None),
        P(("grp", "blk", "rep"), "seq", None),
        P(),
        P(),
        P("seq", None),
        P(("grp", "blk", "rep"), None),
        P(("grp", "blk"), None),
        P(("grp", "blk"), None),
    )
    return jax.shard_map(
        shards,
        mesh=mesh,
        in_specs=placed,
        out_specs=(
            P(("grp", "blk", "rep"), "seq", None),
            P(("grp", "blk", "rep"), "seq", None),
            P(("grp", "blk", "rep"), "seq", None),
            P(("grp", "seq"), None),
            P(("grp", "blk")),
            P("grp"),
        ),
        check_vma=False,
    )
```
